32 devices in a mesh: tm: 4 (over y, x), clus: 8 (over z, core).
Axes of the slice: x: 2, y: 2, z: 4, core: 2. Of those that a mesh axis runs over, the one named last changes fastest.
Arguments:
- embedding: bfloat16 [32768, 384], P(('tm', 'clus')), may hold values from -6 to 6
- cluster_of: int32 [32768], P(('tm', 'clus')), may hold values from 0 to 63, as said below
Outputs:
- mixed: bfloat16 [32768, 384], P(('tm', 'clus'))
The draws below stay inside these ranges and needn't reach their ends.
Inputs may be any that keep to these rules, and one draw needn't show every extreme that they name: `cluster_of`: of the 1024 invoices of one device at most 64 belong to the two clusters of one owner, and on every device some owner receives exactly 64; each cluster holds at most 1024 invoices, and in every draw both clusters of some owner hold exactly 1024.
All inputs are finite; a program needn't handle non-finite values.
Results may differ from the reference program's by a relative error of at most 0.0035.
Values may be sent and summed in bfloat16 or wider, within the bound.
No kernel may reach another device: no remote copies, remote signals or barrier semaphores. Data moves between devices by JAX's collectives and lax.ppermute only.
A program may use at most 64 MiB of HBM per device.

```python
import jax
import jax.numpy as jnp
from jax import lax

E = 384
ROWS_DEV = 1024
OWNERS = 32
NCL = 64
SLOT = 64
CAP = 1024
TOKENS = 32768


def draw_cluster_of(key, part):
    key = jax.random.fold_in(key, 11)
    half = OWNERS // 2
    share = SLOT // 2
    key_pair, key_pick, key_sign, key_full, key_split, key_order = jax.random.split(key, 6)
    offset = jax.random.randint(key_pair, (OWNERS, half), -share, share + 1)
    picked = jax.random.randint(key_pick, (OWNERS,), 0, half)
    signs = jax.random.randint(key_sign, (OWNERS,), 0, 2) * 2 - 1
    columns = jnp.arange(half)[None, :]
    offset = jnp.where(columns == picked[:, None], signs[:, None] * share, offset)
    fullest = jax.random.randint(key_full, (), 0, OWNERS)
    full_sign = jnp.where(fullest < half, 1, -1)
    offset = jnp.where(columns == fullest % half, full_sign * share, offset)
    counts = jnp.concatenate([share + offset, share - offset], axis=1)
    lowest = jnp.maximum(counts - share, 0)
    highest = jnp.minimum(counts, share)
    spread = jax.random.randint(key_split, (OWNERS, OWNERS), 0, 1 << 20)
    first = lowest + spread % (highest - lowest + 1)
    ends = jnp.cumsum(counts, axis=1)
    starts = ends - counts
    places = jnp.arange(ROWS_DEV)
    owner = jax.vmap(lambda edge: jnp.searchsorted(edge, places, side='right'))(ends)
    within = places[None, :] - jnp.take_along_axis(starts, owner, axis=1)
    second = (within >= jnp.take_along_axis(first, owner, axis=1)).astype(jnp.int32)
    cluster = (owner * 2 + second).astype(jnp.int32)
    shuffles = jax.vmap(lambda sub: jax.random.permutation(sub, ROWS_DEV))(jax.random.split(key_order, OWNERS))
    cluster = jnp.take_along_axis(cluster, shuffles, axis=1)
    return cluster.reshape(TOKENS).astype(jnp.int32)


def steps_of(key, shape, pieces, least, high):
    def one(dim, blocks):
        draws = jax.random.uniform(jax.random.fold_in(jax.random.fold_in(key, 6), dim), (blocks,), jnp.float32, least / len(pieces), high / len(pieces))
        return jnp.repeat(jnp.exp(draws), shape[dim] // blocks).reshape((-1,) + (1,) * (len(shape) - dim - 1))

    factor_of = one(*pieces[0])
    for cut in pieces[1:]:
        factor_of = factor_of * one(*cut)
    return factor_of


def scatter_about(key, shape, deviation, reach, shards=(), kind=jnp.bfloat16):
    level = steps_of(key, shape, shards, -0.22, 0.18) if shards else 1.0
    drawn = jax.random.normal(key, shape, jnp.float32) * deviation * level
    return jnp.minimum(jnp.maximum(drawn, -reach), reach).astype(kind)


def setup_inputs(seed: int = 0) -> dict:
    keys = jax.random.split(jax.random.key(seed), 3)
    return {
        "embedding": scatter_about(keys[0], (TOKENS, E), 1.0, 6.0, ((0, 32),)),
        "cluster_of": draw_cluster_of(jax.random.fold_in(keys[2], 71), 0),
    }


TAU = 40.0

def unit_rows(rows):
    values = rows.astype(jnp.float32)
    return (values * lax.rsqrt(lax.optimization_barrier(jnp.sum(values * values, axis=1, keepdims=True)) + 1e-06)).astype(jnp.bfloat16)

def cluster_result(rows, units, present, count, use_skip):
    capacity, width = rows.shape
    block = capacity // 4
    totals = [jnp.zeros((block, width), jnp.float32) for index in range(4)]
    masses = [jnp.zeros((block,), jnp.float32) for index in range(4)]
    inner = jnp.arange(block, dtype=jnp.int32)
    for left in range(4):
        for right in range(left, 4):
            units_left = units[left * block:(left + 1) * block]
            units_right = units[right * block:(right + 1) * block]
            rows_left = rows[left * block:(left + 1) * block]
            rows_right = rows[right * block:(right + 1) * block]
            keep = present[left * block:(left + 1) * block][:, None] & present[right * block:(right + 1) * block][None, :]
            if left == right:
                keep = keep & (inner[:, None] != inner[None, :])

            def scored(unused, units_left=units_left, units_right=units_right, rows_left=rows_left, rows_right=rows_right, keep=keep, diagonal=left == right):
                scores = jnp.dot(units_left, units_right.T, preferred_element_type=jnp.float32)
                weight = jnp.where(keep, jnp.exp(TAU * scores), jnp.zeros((), jnp.float32)).astype(jnp.bfloat16)
                wide = weight.astype(jnp.float32)
                total_left = jnp.dot(weight, rows_right, preferred_element_type=jnp.float32)
                mass_left = lax.optimization_barrier(jnp.sum(wide, axis=1))
                if diagonal:
                    return (total_left, mass_left, jnp.zeros_like(total_left), jnp.zeros_like(mass_left))
                total_right = lax.dot_general(weight, rows_left, (((0,), (0,)), ((), ())), preferred_element_type=jnp.float32)
                return (total_left, mass_left, total_right, lax.optimization_barrier(jnp.sum(wide, axis=0)))

            def skipped(unused):
                empty = jnp.zeros((block, width), jnp.float32)
                none = jnp.zeros((block,), jnp.float32)
                return (empty, none, empty, none)
            if use_skip:
                parts = lax.cond(count > right * block, scored, skipped, None)
            else:
                parts = scored(None)
            totals[left] = totals[left] + parts[0]
            masses[left] = masses[left] + parts[1]
            if left != right:
                totals[right] = totals[right] + parts[2]
                masses[right] = masses[right] + parts[3]
    total = jnp.concatenate(totals, axis=0)
    mass = jnp.concatenate(masses, axis=0)
    return (rows.astype(jnp.float32) - total / (1.0 + mass)[:, None]).astype(jnp.bfloat16)

def reference(embedding, cluster_of):
    total_rows = embedding.shape[0]
    order = jnp.argsort(cluster_of, stable=True).astype(jnp.int32)
    counts = jax.ops.segment_sum(jnp.ones((total_rows,), jnp.int32), cluster_of, num_segments=NCL).astype(jnp.int32)
    starts = (jnp.cumsum(counts) - counts).astype(jnp.int32)
    units = unit_rows(embedding)
    sorted_rows = embedding[order]
    sorted_units = units[order]
    slots = jnp.arange(CAP, dtype=jnp.int32)

    def visit(cluster, result):
        index = starts[cluster] + slots
        present = slots < counts[cluster]
        safe = jnp.minimum(index, total_rows - 1).astype(jnp.int32)
        rows = jnp.where(present[:, None], sorted_rows[safe], jnp.zeros((), embedding.dtype))
        units_here = jnp.where(present[:, None], sorted_units[safe], jnp.zeros((), units.dtype))
        mixed = cluster_result(rows, units_here, present, counts[cluster], True)
        target = jnp.where(present, order[safe], total_rows).astype(jnp.int32)
        return result.at[target].set(mixed.astype(result.dtype), mode='drop')
    return lax.fori_loop(0, NCL, visit, jnp.zeros_like(embedding))
```

```python
import functools
import math

import jax
import jax.numpy as jnp
from jax import lax
from jax.experimental import pallas as pl
from jax.experimental.pallas import tpu as pltpu
from jax.sharding import PartitionSpec as P

TAU = 40.0
LANES = 128
HEAD = 8
BLOCK = 512
VMEM_LIMIT = 32 * 1024 * 1024


def one_hot(mask):
    return jnp.where(mask, 1.0, 0.0).astype(jnp.bfloat16)


def copies_of(source_ref, target_ref, semaphores):
    pieces = semaphores.shape[0]
    each = source_ref.shape[0] // pieces
    spans = [pl.ds(i * each, each) for i in range(pieces)]
    return [
        pltpu.make_async_copy(source_ref.at[span], target_ref.at[span], semaphores.at[i])
        for i, span in enumerate(spans)
    ]


def route_kernel(
    owners, slot, half, cluster_hbm_ref, rows_hbm_ref, out_ref, column_ref,
    cluster_ref, rows_ref, cluster_arrival, rows_arrival,
):
    ids_copy = pltpu.make_async_copy(cluster_hbm_ref, cluster_ref, cluster_arrival)
    ids_copy.start()
    rows_copies = copies_of(rows_hbm_ref, rows_ref, rows_arrival)
    for copy in rows_copies:
        copy.start()
    groups = cluster_ref.shape[0]
    planes = rows_ref.shape[1] // LANES
    ids_copy.wait()
    cluster = cluster_ref[...]
    owner = cluster // 2
    low, side = owner % half, (owner // half) % 2
    cluster = 2 * (owner - low - side * half + 2 * low + side) + cluster % 2
    ids = lax.broadcasted_iota(jnp.int32, (2 * owners, LANES), 0)
    members = [ids == cluster[g : g + 1, :] for g in range(groups)]
    before = lax.broadcasted_iota(jnp.int32, (LANES, 2 * LANES), 0)
    lane = lax.broadcasted_iota(jnp.int32, (LANES, 2 * LANES), 1)
    counter = one_hot((before < lane) | (lane >= LANES))
    odd = ids % 2 == 1
    start = ((ids // 2) * slot + jnp.where(odd, slot - 1, 0)).astype(jnp.float32)
    total = jnp.zeros(ids.shape, jnp.float32)
    targets = []
    for g in range(groups):
        counted = jnp.dot(one_hot(members[g]), counter, preferred_element_type=jnp.float32)
        rank = counted[:, :LANES] + total
        place = start + jnp.where(odd, -rank, rank)
        targets.append(jnp.sum(jnp.where(members[g], place, 0.0), axis=0, keepdims=True))
        total = total + counted[:, LANES:]
    target = jnp.concatenate(targets, axis=0)
    column_ref[...] = target.T.astype(jnp.int32)
    target = target.astype(jnp.int32)
    upper = lax.broadcasted_iota(jnp.int32, (HEAD, LANES), 0) < HEAD // 2
    for o in range(owners):
        out_ref[o, planes * slot :, :] = jnp.where(
            upper, total[2 * o : 2 * o + 1, :], total[2 * o + 1 : 2 * o + 2, :]
        ).astype(jnp.bfloat16)
    for copy in rows_copies:
        copy.wait()
    for b in range(owners * slot // BLOCK):
        places = lax.broadcasted_iota(jnp.int32, (BLOCK, LANES), 0) + b * BLOCK
        pick = jnp.concatenate(
            [one_hot(places == target[g : g + 1, :]) for g in range(groups)], axis=1
        )
        sent = jnp.dot(pick, rows_ref[...], preferred_element_type=jnp.float32)
        sent = sent.astype(jnp.bfloat16)
        first, count = b * BLOCK // slot, BLOCK // slot
        for j in range(planes):
            out_ref[first : first + count, j * slot : (j + 1) * slot, :] = sent[
                :, j * LANES : (j + 1) * LANES
            ].reshape(count, slot, LANES)


def weights(left, right, diagonal):
    scores = lax.dot_general(
        left, right, (((1,), (1,)), ((), ())), preferred_element_type=jnp.float32
    )
    weight = jnp.exp2(scores * (TAU * math.log2(math.e)))
    if diagonal:
        here = lax.broadcasted_iota(jnp.int32, (BLOCK, BLOCK), 0)
        there = lax.broadcasted_iota(jnp.int32, (BLOCK, BLOCK), 1)
        weight = jnp.where(here == there, 0.0, weight)
    return weight.astype(jnp.bfloat16)


def summed(weight, value, transposed=False):
    return lax.dot_general(
        weight,
        value,
        (((0 if transposed else 1,), (0,)), ((), ())),
        preferred_element_type=jnp.float32,
    )


def owner_kernel(owners, slot, rows_ref, out_ref, unit_ref, value_ref, left_ref, right_ref):
    size, width = unit_ref.shape
    planes = width // LANES
    part = slot // 2
    side = size // 2
    lane = lax.broadcasted_iota(jnp.int32, (part, LANES), 1)
    rank = lax.broadcasted_iota(jnp.int32, (part, LANES), 0).astype(jnp.float32)
    most = jnp.zeros((HEAD, LANES), jnp.float32)

    def counts_of(s):
        counts = rows_ref[s, planes * slot :, :].astype(jnp.float32)
        return counts, counts[:1, :], counts[HEAD // 2 : HEAD // 2 + 1, :]

    for s in range(owners):
        counts, first, second = counts_of(s)
        most = jnp.maximum(most, counts)
        for h in range(2):
            here = pl.ds(h * side + s * part, part)
            there = (rank + h * part < first) | (rank + h * part >= slot - second)
            value_ref[here, width:] = one_hot(there & (lane == 0))
            for j in range(planes):
                at = j * slot + h * part
                value_ref[here, j * LANES : (j + 1) * LANES] = rows_ref[s, at : at + part, :]
    for b in range(size // BLOCK):
        span = slice(b * BLOCK, (b + 1) * BLOCK)
        wide = value_ref[span, :width].astype(jnp.float32)
        unit_ref[span, :] = (
            wide * lax.rsqrt(jnp.sum(wide * wide, axis=1, keepdims=True) + 1e-06)
        ).astype(jnp.bfloat16)

    def finish(b, total):
        mass = total[:, width : width + 1]
        span = slice(b * BLOCK, (b + 1) * BLOCK)
        result = value_ref[span, :width].astype(jnp.float32) - total[:, :width] / (1.0 + mass)
        result = result.astype(jnp.bfloat16)
        h, s = b * BLOCK // side, b * BLOCK % side // part
        for i in range(BLOCK // part):
            at = (s + i) * slot + h * part
            out_ref[at : at + part, :] = result[i * part : (i + 1) * part, :]

    blocks = side // BLOCK
    spans = [slice(b * BLOCK, (b + 1) * BLOCK) for b in range(2 * blocks)]
    for h in range(2):
        mine = range(h * blocks, (h + 1) * blocks)
        totals = {b: 0.0 for b in mine}
        for b in mine:
            for k in range(b, mine[-1] + 1):
                weight = weights(unit_ref[spans[b], :], unit_ref[spans[k], :], b == k)
                totals[b] = totals[b] + summed(weight, value_ref[spans[k], :])
                if k != b:
                    totals[k] = totals[k] + summed(weight, value_ref[spans[b], :], True)
            finish(b, totals[b])

    @pl.when(jnp.max(most) > part)
    def all_pairs():
        for s in range(owners):
            counts, first, second = counts_of(s)
            for h in range(2):
                here = pl.ds(h * side + s * part, part)
                sign = jnp.where(rank + h * part < first, 1.0, -1.0)
                left = jnp.where(lane == 0, sign, jnp.where(lane == 1, 1.0, 0.0))
                right = jnp.where(lane == 0, 2.0 * sign, jnp.where(lane == 1, -2.0, 0.0))
                left_ref[here, width:] = left.astype(jnp.bfloat16)
                right_ref[here, width:] = right.astype(jnp.bfloat16)
        left_ref[:, :width] = unit_ref[...]
        right_ref[:, :width] = unit_ref[...]
        for b in range(2 * blocks):
            total = 0.0
            for k in range(2 * blocks):
                weight = weights(left_ref[spans[b], :], right_ref[spans[k], :], b == k)
                total = total + summed(weight, value_ref[spans[k], :])
            finish(b, total)


def return_kernel(column_ref, rows_ref, out_ref, held_ref, leaving):
    column = column_ref[...]
    places = lax.broadcasted_iota(jnp.int32, (LANES, rows_ref.shape[0]), 1)
    each = BLOCK // LANES
    copies = copies_of(held_ref, out_ref, leaving)
    ready = len(copies) * BLOCK // held_ref.shape[0]
    for b in range(column.shape[1] // each):
        pick = jnp.concatenate(
            [one_hot(places == column[:, g : g + 1]) for g in range(b * each, (b + 1) * each)],
            axis=0,
        )
        held_ref[b * BLOCK : (b + 1) * BLOCK, :] = jnp.dot(
            pick, rows_ref[...], preferred_element_type=jnp.float32
        ).astype(jnp.bfloat16)
        for copy in copies[b * ready : (b + 1) * ready]:
            copy.start()
    for copy in copies:
        copy.wait()


VMEM = pl.BlockSpec(memory_space=pltpu.VMEM)
HBM = pl.BlockSpec(memory_space=pltpu.HBM)
PARAMS = pltpu.CompilerParams(vmem_limit_bytes=VMEM_LIMIT)


def on_device(embedding, cluster_of):
    rows_here, width = embedding.shape
    axes = ("tm", "clus")
    owners = lax.axis_size("tm") * lax.axis_size("clus")
    half = lax.axis_size("clus") // 2
    slot = 2 * rows_here // owners
    size = owners * slot
    groups = rows_here // LANES
    padded = width + LANES
    depth = slot * (width // LANES) + HEAD
    outgoing, column = pl.pallas_call(
        functools.partial(route_kernel, owners, slot, half),
        out_shape=(
            jax.ShapeDtypeStruct((owners, depth, LANES), jnp.bfloat16),
            jax.ShapeDtypeStruct((LANES, groups), jnp.int32),
        ),
        in_specs=[HBM, HBM],
        out_specs=(VMEM, VMEM),
        scratch_shapes=[
            pltpu.VMEM((groups, LANES), jnp.int32),
            pltpu.VMEM((rows_here, width), jnp.bfloat16),
            pltpu.SemaphoreType.DMA,
            pltpu.SemaphoreType.DMA((4,)),
        ],
        compiler_params=PARAMS,
        name="route",
    )(
        pltpu.with_memory_space_constraint(cluster_of.reshape(groups, LANES), pltpu.HBM),
        pltpu.with_memory_space_constraint(embedding, pltpu.HBM),
    )

    order = [
        start + side * half + low
        for start in range(0, owners, 2 * half)
        for low in range(half)
        for side in range(2)
    ]

    def exchange(rows):
        return lax.all_to_all(
            rows, axes, split_axis=0, concat_axis=0, tiled=True, axis_index_groups=[order]
        )

    arrived = exchange(outgoing)
    answers = pl.pallas_call(
        functools.partial(owner_kernel, owners, slot),
        out_shape=jax.ShapeDtypeStruct((size, width), jnp.bfloat16),
        in_specs=[VMEM],
        out_specs=VMEM,
        scratch_shapes=[pltpu.VMEM((size, width), jnp.bfloat16)]
        + [pltpu.VMEM((size, padded), jnp.bfloat16)] * 3,
        compiler_params=PARAMS,
        name="pairs",
    )(arrived)
    returned = exchange(answers.reshape(owners, slot, width)).reshape(size, width)
    return pl.pallas_call(
        return_kernel,
        out_shape=jax.ShapeDtypeStruct((rows_here, width), jnp.bfloat16),
        in_specs=[VMEM, VMEM],
        out_specs=pl.BlockSpec(memory_space=pl.ANY),
        scratch_shapes=[
            pltpu.VMEM((rows_here, width), jnp.bfloat16),
            pltpu.SemaphoreType.DMA((8,)),
        ],
        compiler_params=PARAMS,
        name="back",
    )(column, returned)


def solution(mesh):
    return jax.shard_map(
        on_device,
        mesh=mesh,
        in_specs=(P(("tm", "clus"), None), P(("tm", "clus"))),
        out_specs=P(("tm", "clus"), None),
        check_vma=False,
    )
```

```python
import functools
import math

import jax
import jax.numpy as jnp
from jax import lax
from jax.experimental import pallas as pl
from jax.experimental.pallas import tpu as pltpu
from jax.sharding import PartitionSpec as P

TAU = 40.0
LANES = 128
HEAD = 8
BLOCK = 512
TILE = 256
VMEM_LIMIT = 32 * 1024 * 1024


def one_hot(mask):
    return jnp.where(mask, 1.0, 0.0).astype(jnp.bfloat16)


def copies_of(source_ref, target_ref, semaphores):
    pieces = semaphores.shape[0]
    each = source_ref.shape[0] // pieces
    spans = [pl.ds(i * each, each) for i in range(pieces)]
    return [
        pltpu.make_async_copy(source_ref.at[span], target_ref.at[span], semaphores.at[i])
        for i, span in enumerate(spans)
    ]


def route_kernel(
    owners, slot, half, cluster_hbm_ref, rows_hbm_ref, out_ref, column_ref,
    cluster_ref, rows_ref, cluster_arrival, rows_arrival,
):
    ids_copy = pltpu.make_async_copy(cluster_hbm_ref, cluster_ref, cluster_arrival)
    ids_copy.start()
    rows_copies = copies_of(rows_hbm_ref, rows_ref, rows_arrival)
    for copy in rows_copies:
        copy.start()
    groups = cluster_ref.shape[0]
    planes = rows_ref.shape[1] // LANES
    ids_copy.wait()
    cluster = cluster_ref[...]
    owner = cluster // 2
    low, side = owner % half, (owner // half) % 2
    cluster = 2 * (owner - low - side * half + 2 * low + side) + cluster % 2
    ids = lax.broadcasted_iota(jnp.int32, (2 * owners, LANES), 0)
    members = [ids == cluster[g : g + 1, :] for g in range(groups)]
    before = lax.broadcasted_iota(jnp.int32, (LANES, 2 * LANES), 0)
    lane = lax.broadcasted_iota(jnp.int32, (LANES, 2 * LANES), 1)
    counter = one_hot((before < lane) | (lane >= LANES))
    odd = ids % 2 == 1
    start = ((ids // 2) * slot + jnp.where(odd, slot - 1, 0)).astype(jnp.float32)
    total = jnp.zeros(ids.shape, jnp.float32)
    targets = []
    for g in range(groups):
        counted = jnp.dot(one_hot(members[g]), counter, preferred_element_type=jnp.float32)
        rank = counted[:, :LANES] + total
        place = start + jnp.where(odd, -rank, rank)
        targets.append(jnp.sum(jnp.where(members[g], place, 0.0), axis=0, keepdims=True))
        total = total + counted[:, LANES:]
    target = jnp.concatenate(targets, axis=0)
    column_ref[...] = target.T.astype(jnp.int32)
    target = target.astype(jnp.int32)
    upper = lax.broadcasted_iota(jnp.int32, (HEAD, LANES), 0) < HEAD // 2
    for o in range(owners):
        out_ref[o, planes * slot :, :] = jnp.where(
            upper, total[2 * o : 2 * o + 1, :], total[2 * o + 1 : 2 * o + 2, :]
        ).astype(jnp.bfloat16)
    for copy in rows_copies:
        copy.wait()
    for b in range(owners * slot // BLOCK):
        places = lax.broadcasted_iota(jnp.int32, (BLOCK, LANES), 0) + b * BLOCK
        pick = jnp.concatenate(
            [one_hot(places == target[g : g + 1, :]) for g in range(groups)], axis=1
        )
        sent = jnp.dot(pick, rows_ref[...], preferred_element_type=jnp.float32)
        sent = sent.astype(jnp.bfloat16)
        first, count = b * BLOCK // slot, BLOCK // slot
        for j in range(planes):
            out_ref[first : first + count, j * slot : (j + 1) * slot, :] = sent[
                :, j * LANES : (j + 1) * LANES
            ].reshape(count, slot, LANES)


def weights(left, right, diagonal):
    scores = lax.dot_general(
        left, right, (((1,), (1,)), ((), ())), preferred_element_type=jnp.float32
    )
    weight = jnp.exp2(scores * (TAU * math.log2(math.e)))
    if diagonal:
        here = lax.broadcasted_iota(jnp.int32, weight.shape, 0)
        there = lax.broadcasted_iota(jnp.int32, weight.shape, 1)
        weight = jnp.where(here == there, 0.0, weight)
    return weight.astype(jnp.bfloat16)


def owner_kernel(
    owners, slot, rows_ref, out_ref, unit_ref, value_ref, left_ref, right_ref, *weight_refs
):
    size, width = unit_ref.shape
    planes = width // LANES
    part = slot // 2
    side = size // 2
    lane = lax.broadcasted_iota(jnp.int32, (part, LANES), 1)
    rank = lax.broadcasted_iota(jnp.int32, (part, LANES), 0).astype(jnp.float32)
    most = jnp.zeros((HEAD, LANES), jnp.float32)

    def counts_of(s):
        counts = rows_ref[s, planes * slot :, :].astype(jnp.float32)
        return counts, counts[:1, :], counts[HEAD // 2 : HEAD // 2 + 1, :]

    for s in range(owners):
        counts, first, second = counts_of(s)
        most = jnp.maximum(most, counts)
        for h in range(2):
            here = pl.ds(h * side + s * part, part)
            there = (rank + h * part < first) | (rank + h * part >= slot - second)
            value_ref[here, width:] = one_hot(there & (lane == 0))
            for j in range(planes):
                at = j * slot + h * part
                value_ref[here, j * LANES : (j + 1) * LANES] = rows_ref[s, at : at + part, :]
    for b in range(size // BLOCK):
        span = slice(b * BLOCK, (b + 1) * BLOCK)
        wide = value_ref[span, :width].astype(jnp.float32)
        unit_ref[span, :] = (
            wide * lax.rsqrt(jnp.sum(wide * wide, axis=1, keepdims=True) + 1e-06)
        ).astype(jnp.bfloat16)

    def finish(b, total):
        mass = total[:, width : width + 1]
        span = slice(b * BLOCK, (b + 1) * BLOCK)
        result = value_ref[span, :width].astype(jnp.float32) - total[:, :width] / (1.0 + mass)
        result = result.astype(jnp.bfloat16)
        h, s = b * BLOCK // side, b * BLOCK % side // part
        for i in range(BLOCK // part):
            at = (s + i) * slot + h * part
            out_ref[at : at + part, :] = result[i * part : (i + 1) * part, :]

    blocks = side // BLOCK
    spans = [slice(b * BLOCK, (b + 1) * BLOCK) for b in range(2 * blocks)]
    tiles = [slice(at, at + TILE) for at in range(0, side, TILE)]
    for h in range(2):
        weight_ref = weight_refs[h]
        units = [unit_ref[h * side + t.start : h * side + t.stop, :] for t in tiles]
        for k, across in enumerate(tiles):
            for b, down in enumerate(tiles[: k + 1]):
                weight = weights(units[b], units[k], b == k)
                weight_ref[down, across] = weight
                if b != k:
                    weight_ref[across, down] = weight.T
        for b in range(blocks):
            total = jnp.dot(
                weight_ref[spans[b], :],
                value_ref[h * side : (h + 1) * side, :],
                preferred_element_type=jnp.float32,
            )
            finish(h * blocks + b, total)

    @pl.when(jnp.max(most) > part)
    def all_pairs():
        for s in range(owners):
            counts, first, second = counts_of(s)
            for h in range(2):
                here = pl.ds(h * side + s * part, part)
                sign = jnp.where(rank + h * part < first, 1.0, -1.0)
                left = jnp.where(lane == 0, sign, jnp.where(lane == 1, 1.0, 0.0))
                right = jnp.where(lane == 0, 2.0 * sign, jnp.where(lane == 1, -2.0, 0.0))
                left_ref[here, width:] = left.astype(jnp.bfloat16)
                right_ref[here, width:] = right.astype(jnp.bfloat16)
        left_ref[:, :width] = unit_ref[...]
        right_ref[:, :width] = unit_ref[...]
        for b in range(2 * blocks):
            total = 0.0
            for k in range(2 * blocks):
                weight = weights(left_ref[spans[b], :], right_ref[spans[k], :], b == k)
                total = total + jnp.dot(
                    weight, value_ref[spans[k], :], preferred_element_type=jnp.float32
                )
            finish(b, total)


def return_kernel(column_ref, rows_ref, out_ref, held_ref, leaving):
    column = column_ref[...]
    places = lax.broadcasted_iota(jnp.int32, (LANES, rows_ref.shape[0]), 1)
    each = BLOCK // LANES
    copies = copies_of(held_ref, out_ref, leaving)
    ready = len(copies) * BLOCK // held_ref.shape[0]
    for b in range(column.shape[1] // each):
        pick = jnp.concatenate(
            [one_hot(places == column[:, g : g + 1]) for g in range(b * each, (b + 1) * each)],
            axis=0,
        )
        held_ref[b * BLOCK : (b + 1) * BLOCK, :] = jnp.dot(
            pick, rows_ref[...], preferred_element_type=jnp.float32
        ).astype(jnp.bfloat16)
        for copy in copies[b * ready : (b + 1) * ready]:
            copy.start()
    for copy in copies:
        copy.wait()


VMEM = pl.BlockSpec(memory_space=pltpu.VMEM)
HBM = pl.BlockSpec(memory_space=pltpu.HBM)
PARAMS = pltpu.CompilerParams(vmem_limit_bytes=VMEM_LIMIT)


def on_device(embedding, cluster_of):
    rows_here, width = embedding.shape
    axes = ("tm", "clus")
    owners = lax.axis_size("tm") * lax.axis_size("clus")
    half = lax.axis_size("clus") // 2
    slot = 2 * rows_here // owners
    size = owners * slot
    groups = rows_here // LANES
    padded = width + LANES
    depth = slot * (width // LANES) + HEAD
    outgoing, column = pl.pallas_call(
        functools.partial(route_kernel, owners, slot, half),
        out_shape=(
            jax.ShapeDtypeStruct((owners, depth, LANES), jnp.bfloat16),
            jax.ShapeDtypeStruct((LANES, groups), jnp.int32),
        ),
        in_specs=[HBM, HBM],
        out_specs=(VMEM, VMEM),
        scratch_shapes=[
            pltpu.VMEM((groups, LANES), jnp.int32),
            pltpu.VMEM((rows_here, width), jnp.bfloat16),
            pltpu.SemaphoreType.DMA,
            pltpu.SemaphoreType.DMA((4,)),
        ],
        compiler_params=PARAMS,
        name="route",
    )(
        pltpu.with_memory_space_constraint(cluster_of.reshape(groups, LANES), pltpu.HBM),
        pltpu.with_memory_space_constraint(embedding, pltpu.HBM),
    )

    order = [
        start + side * half + low
        for start in range(0, owners, 2 * half)
        for low in range(half)
        for side in range(2)
    ]

    def exchange(rows):
        return lax.all_to_all(
            rows, axes, split_axis=0, concat_axis=0, tiled=True, axis_index_groups=[order]
        )

    arrived = exchange(outgoing)
    answers = pl.pallas_call(
        functools.partial(owner_kernel, owners, slot),
        out_shape=jax.ShapeDtypeStruct((size, width), jnp.bfloat16),
        in_specs=[VMEM],
        out_specs=VMEM,
        scratch_shapes=[pltpu.VMEM((size, width), jnp.bfloat16)]
        + [pltpu.VMEM((size, padded), jnp.bfloat16)] * 3
        + [pltpu.VMEM((size // 2, size // 2), jnp.bfloat16)] * 2,
        compiler_params=PARAMS,
        name="pairs",
    )(arrived)
    returned = exchange(answers.reshape(owners, slot, width)).reshape(size, width)
    return pl.pallas_call(
        return_kernel,
        out_shape=jax.ShapeDtypeStruct((rows_here, width), jnp.bfloat16),
        in_specs=[VMEM, VMEM],
        out_specs=pl.BlockSpec(memory_space=pl.ANY),
        scratch_shapes=[
            pltpu.VMEM((rows_here, width), jnp.bfloat16),
            pltpu.SemaphoreType.DMA((8,)),
        ],
        compiler_params=PARAMS,
        name="back",
    )(column, returned)


def solution(mesh):
    return jax.shard_map(
        on_device,
        mesh=mesh,
        in_specs=(P(("tm", "clus"), None), P(("tm", "clus"))),
        out_specs=P(("tm", "clus"), None),
        check_vma=False,
    )
```

```python
import functools
import math

import jax
import jax.numpy as jnp
from jax import lax
from jax.experimental import pallas as pl
from jax.experimental.pallas import tpu as pltpu
from jax.sharding import PartitionSpec as P

TAU = 40.0
LANES = 128
HEAD = 8
BLOCK = 512
TILE = 256
VMEM_LIMIT = 32 * 1024 * 1024


def one_hot(mask):
    return jnp.where(mask, 1.0, 0.0).astype(jnp.bfloat16)


def copies_of(source_ref, target_ref, semaphores):
    pieces = semaphores.shape[0]
    each = source_ref.shape[0] // pieces
    spans = [pl.ds(i * each, each) for i in range(pieces)]
    return [
        pltpu.make_async_copy(source_ref.at[span], target_ref.at[span], semaphores.at[i])
        for i, span in enumerate(spans)
    ]


def route_kernel(
    owners, slot, half, cluster_hbm_ref, rows_hbm_ref, out_ref, target_ref,
    cluster_ref, rows_ref, turned_ref, cluster_arrival, rows_arrival,
):
    ids_copy = pltpu.make_async_copy(cluster_hbm_ref, cluster_ref, cluster_arrival)
    ids_copy.start()
    rows_copies = copies_of(rows_hbm_ref, rows_ref, rows_arrival)
    for copy in rows_copies:
        copy.start()
    groups = cluster_ref.shape[0]
    planes = rows_ref.shape[1] // LANES
    ids_copy.wait()
    cluster = cluster_ref[...]
    owner = cluster // 2
    low, side = owner % half, (owner // half) % 2
    cluster = 2 * (owner - low - side * half + 2 * low + side) + cluster % 2
    ids = lax.broadcasted_iota(jnp.int32, (2 * owners, LANES), 0)
    members = [ids == cluster[g : g + 1, :] for g in range(groups)]
    before = lax.broadcasted_iota(jnp.int32, (LANES, 2 * LANES), 0)
    lane = lax.broadcasted_iota(jnp.int32, (LANES, 2 * LANES), 1)
    counter = one_hot((before < lane) | (lane >= LANES))
    odd = ids % 2 == 1
    start = ((ids // 2) * slot + jnp.where(odd, slot - 1, 0)).astype(jnp.float32)
    total = jnp.zeros(ids.shape, jnp.float32)
    targets = []
    for g in range(groups):
        counted = jnp.dot(one_hot(members[g]), counter, preferred_element_type=jnp.float32)
        rank = counted[:, :LANES] + total
        place = start + jnp.where(odd, -rank, rank)
        targets.append(jnp.sum(jnp.where(members[g], place, 0.0), axis=0, keepdims=True))
        total = total + counted[:, LANES:]
    target = jnp.concatenate(targets, axis=0)
    target = target.astype(jnp.int32)
    target_ref[...] = target
    upper = lax.broadcasted_iota(jnp.int32, (HEAD, LANES), 0) < HEAD // 2
    for o in range(owners):
        out_ref[o, planes * slot :, :] = jnp.where(
            upper, total[2 * o : 2 * o + 1, :], total[2 * o + 1 : 2 * o + 2, :]
        ).astype(jnp.bfloat16)
    for copy in rows_copies:
        copy.wait()
    for at in range(0, rows_ref.shape[0], BLOCK):
        turned_ref[:, at : at + BLOCK] = rows_ref[at : at + BLOCK, :].T
    for b in range(owners * slot // BLOCK):
        places = lax.broadcasted_iota(jnp.int32, (BLOCK, LANES), 0) + b * BLOCK
        pick = jnp.concatenate(
            [one_hot(places == target[g : g + 1, :]) for g in range(groups)], axis=1
        )
        sent = lax.dot_general(
            turned_ref[...], pick, (((1,), (1,)), ((), ())), preferred_element_type=jnp.float32
        )
        sent = sent.astype(jnp.bfloat16).T
        first, count = b * BLOCK // slot, BLOCK // slot
        for j in range(planes):
            out_ref[first : first + count, j * slot : (j + 1) * slot, :] = sent[
                :, j * LANES : (j + 1) * LANES
            ].reshape(count, slot, LANES)


def weights(left, right, diagonal):
    scores = lax.dot_general(
        left, right, (((1,), (1,)), ((), ())), preferred_element_type=jnp.float32
    )
    weight = jnp.exp2(scores * (TAU * math.log2(math.e)))
    if diagonal:
        here = lax.broadcasted_iota(jnp.int32, weight.shape, 0)
        there = lax.broadcasted_iota(jnp.int32, weight.shape, 1)
        weight = jnp.where(here == there, 0.0, weight)
    return weight.astype(jnp.bfloat16)


def owner_kernel(
    owners, slot, rows_ref, out_ref, unit_ref, value_ref, left_ref, right_ref, *refs
):
    size, width = unit_ref.shape
    planes = width // LANES
    part = slot // 2
    side = size // 2
    lane = lax.broadcasted_iota(jnp.int32, (part, LANES), 1)
    rank = lax.broadcasted_iota(jnp.int32, (part, LANES), 0).astype(jnp.float32)
    most = jnp.zeros((HEAD, LANES), jnp.float32)

    def counts_of(s):
        counts = rows_ref[s, planes * slot :, :].astype(jnp.float32)
        return counts, counts[:1, :], counts[HEAD // 2 : HEAD // 2 + 1, :]

    for s in range(owners):
        counts, first, second = counts_of(s)
        most = jnp.maximum(most, counts)
        for h in range(2):
            here = pl.ds(h * side + s * part, part)
            there = (rank + h * part < first) | (rank + h * part >= slot - second)
            value_ref[here, width:] = one_hot(there & (lane == 0))
            for j in range(planes):
                at = j * slot + h * part
                value_ref[here, j * LANES : (j + 1) * LANES] = rows_ref[s, at : at + part, :]
    for b in range(size // BLOCK):
        span = slice(b * BLOCK, (b + 1) * BLOCK)
        wide = value_ref[span, :width].astype(jnp.float32)
        unit_ref[span, :] = (
            wide * lax.rsqrt(jnp.sum(wide * wide, axis=1, keepdims=True) + 1e-06)
        ).astype(jnp.bfloat16)

    def write(b, result):
        h, s = b * BLOCK // side, b * BLOCK % side // part
        for i in range(BLOCK // part):
            at = (s + i) * slot + h * part
            out_ref[at : at + part, :] = result[i * part : (i + 1) * part, :]

    blocks = side // BLOCK
    spans = [slice(b * BLOCK, (b + 1) * BLOCK) for b in range(2 * blocks)]
    tiles = [slice(at, at + TILE) for at in range(0, side, TILE)]
    for h in range(2):
        weight_ref, turned_ref = refs[h], refs[2 + h]
        units = [unit_ref[h * side + t.start : h * side + t.stop, :] for t in tiles]
        for k, across in enumerate(tiles):
            for b, down in enumerate(tiles[: k + 1]):
                weight = weights(units[b], units[k], b == k)
                weight_ref[down, across] = weight
                if b != k:
                    weight_ref[across, down] = weight.T
        for b in range(blocks):
            span = spans[h * blocks + b]
            turned_ref[:width, spans[b]] = value_ref[span, :width].T
            turned_ref[width:, spans[b]] = value_ref[span, width:].T[: 2 * HEAD, :]
        for b in range(blocks):
            total = jnp.dot(
                turned_ref[...], weight_ref[:, spans[b]], preferred_element_type=jnp.float32
            )
            result = turned_ref[:width, spans[b]].astype(jnp.float32)
            result = result - total[:width, :] / (1.0 + total[width : width + 1, :])
            write(h * blocks + b, result.astype(jnp.bfloat16).T)

    @pl.when(jnp.max(most) > part)
    def all_pairs():
        for s in range(owners):
            counts, first, second = counts_of(s)
            for h in range(2):
                here = pl.ds(h * side + s * part, part)
                sign = jnp.where(rank + h * part < first, 1.0, -1.0)
                left = jnp.where(lane == 0, sign, jnp.where(lane == 1, 1.0, 0.0))
                right = jnp.where(lane == 0, 2.0 * sign, jnp.where(lane == 1, -2.0, 0.0))
                left_ref[here, width:] = left.astype(jnp.bfloat16)
                right_ref[here, width:] = right.astype(jnp.bfloat16)
        left_ref[:, :width] = unit_ref[...]
        right_ref[:, :width] = unit_ref[...]
        for b in range(2 * blocks):
            total = 0.0
            for k in range(2 * blocks):
                weight = weights(left_ref[spans[b], :], right_ref[spans[k], :], b == k)
                total = total + jnp.dot(
                    weight, value_ref[spans[k], :], preferred_element_type=jnp.float32
                )
            mass = total[:, width : width + 1]
            result = value_ref[spans[b], :width].astype(jnp.float32)
            write(b, (result - total[:, :width] / (1.0 + mass)).astype(jnp.bfloat16))


def return_kernel(target_ref, rows_ref, out_ref, turned_ref, held_ref, leaving):
    target = target_ref[...]
    size, width = rows_ref.shape
    for at in range(0, size, BLOCK):
        turned_ref[:, at : at + BLOCK] = rows_ref[at : at + BLOCK, :].T
    places = lax.broadcasted_iota(jnp.int32, (size, LANES), 0)
    each = TILE // LANES
    copies = copies_of(held_ref, out_ref, leaving)
    ready = len(copies) * TILE // held_ref.shape[0]
    for b in range(held_ref.shape[0] // TILE):
        pick = jnp.concatenate(
            [one_hot(places == target[g : g + 1, :]) for g in range(b * each, (b + 1) * each)],
            axis=1,
        )
        result = jnp.dot(turned_ref[...], pick, preferred_element_type=jnp.float32)
        held_ref[b * TILE : (b + 1) * TILE, :] = result.astype(jnp.bfloat16).T
        for copy in copies[b * ready : (b + 1) * ready]:
            copy.start()
    for copy in copies:
        copy.wait()


VMEM = pl.BlockSpec(memory_space=pltpu.VMEM)
HBM = pl.BlockSpec(memory_space=pltpu.HBM)
PARAMS = pltpu.CompilerParams(vmem_limit_bytes=VMEM_LIMIT)


def on_device(embedding, cluster_of):
    rows_here, width = embedding.shape
    axes = ("tm", "clus")
    owners = lax.axis_size("tm") * lax.axis_size("clus")
    half = lax.axis_size("clus") // 2
    slot = 2 * rows_here // owners
    size = owners * slot
    groups = rows_here // LANES
    padded = width + LANES
    depth = slot * (width // LANES) + HEAD
    outgoing, target = pl.pallas_call(
        functools.partial(route_kernel, owners, slot, half),
        out_shape=(
            jax.ShapeDtypeStruct((owners, depth, LANES), jnp.bfloat16),
            jax.ShapeDtypeStruct((groups, LANES), jnp.int32),
        ),
        in_specs=[HBM, HBM],
        out_specs=(VMEM, VMEM),
        scratch_shapes=[
            pltpu.VMEM((groups, LANES), jnp.int32),
            pltpu.VMEM((rows_here, width), jnp.bfloat16),
            pltpu.VMEM((width, rows_here), jnp.bfloat16),
            pltpu.SemaphoreType.DMA,
            pltpu.SemaphoreType.DMA((4,)),
        ],
        compiler_params=PARAMS,
        name="route",
    )(
        pltpu.with_memory_space_constraint(cluster_of.reshape(groups, LANES), pltpu.HBM),
        pltpu.with_memory_space_constraint(embedding, pltpu.HBM),
    )

    order = [
        start + side * half + low
        for start in range(0, owners, 2 * half)
        for low in range(half)
        for side in range(2)
    ]

    def exchange(rows):
        return lax.all_to_all(
            rows, axes, split_axis=0, concat_axis=0, tiled=True, axis_index_groups=[order]
        )

    arrived = exchange(outgoing)
    answers = pl.pallas_call(
        functools.partial(owner_kernel, owners, slot),
        out_shape=jax.ShapeDtypeStruct((size, width), jnp.bfloat16),
        in_specs=[VMEM],
        out_specs=VMEM,
        scratch_shapes=[pltpu.VMEM((size, width), jnp.bfloat16)]
        + [pltpu.VMEM((size, padded), jnp.bfloat16)] * 3
        + [pltpu.VMEM((size // 2, size // 2), jnp.bfloat16)] * 2
        + [pltpu.VMEM((width + 2 * HEAD, size // 2), jnp.bfloat16)] * 2,
        compiler_params=PARAMS,
        name="pairs",
    )(arrived)
    returned = exchange(answers.reshape(owners, slot, width)).reshape(size, width)
    return pl.pallas_call(
        return_kernel,
        out_shape=jax.ShapeDtypeStruct((rows_here, width), jnp.bfloat16),
        in_specs=[VMEM, VMEM],
        out_specs=pl.BlockSpec(memory_space=pl.ANY),
        scratch_shapes=[
            pltpu.VMEM((width, size), jnp.bfloat16),
            pltpu.VMEM((rows_here, width), jnp.bfloat16),
            pltpu.SemaphoreType.DMA((8,)),
        ],
        compiler_params=PARAMS,
        name="back",
    )(target, returned)


def solution(mesh):
    return jax.shard_map(
        on_device,
        mesh=mesh,
        in_specs=(P(("tm", "clus"), None), P(("tm", "clus"))),
        out_specs=P(("tm", "clus"), None),
        check_vma=False,
    )
```

```python
import functools
import math

import jax
import jax.numpy as jnp
from jax import lax
from jax.experimental import pallas as pl
from jax.experimental.pallas import tpu as pltpu
from jax.sharding import PartitionSpec as P

TAU = 40.0
LANES = 128
HEAD = 8
BLOCK = 512
TILE = 256
VMEM_LIMIT = 32 * 1024 * 1024


def one_hot(mask):
    return jnp.where(mask, 1.0, 0.0).astype(jnp.bfloat16)


def copies_of(source_ref, target_ref, semaphores):
    pieces = semaphores.shape[0]
    each = source_ref.shape[0] // pieces
    spans = [pl.ds(i * each, each) for i in range(pieces)]
    return [
        pltpu.make_async_copy(source_ref.at[span], target_ref.at[span], semaphores.at[i])
        for i, span in enumerate(spans)
    ]


def route_kernel(
    owners, slot, half, cluster_hbm_ref, rows_hbm_ref, out_ref, target_ref,
    cluster_ref, rows_ref, turned_ref, cluster_arrival, rows_arrival,
):
    ids_copy = pltpu.make_async_copy(cluster_hbm_ref, cluster_ref, cluster_arrival)
    ids_copy.start()
    rows_copies = copies_of(rows_hbm_ref, rows_ref, rows_arrival)
    for copy in rows_copies:
        copy.start()
    groups = cluster_ref.shape[0]
    planes = rows_ref.shape[1] // LANES
    ids_copy.wait()
    cluster = cluster_ref[...]
    owner = cluster // 2
    low, side = owner % half, (owner // half) % 2
    cluster = 2 * (owner - low - side * half + 2 * low + side) + cluster % 2
    ids = lax.broadcasted_iota(jnp.int32, (2 * owners, LANES), 0)
    members = [ids == cluster[g : g + 1, :] for g in range(groups)]
    before = lax.broadcasted_iota(jnp.int32, (LANES, 2 * LANES), 0)
    lane = lax.broadcasted_iota(jnp.int32, (LANES, 2 * LANES), 1)
    counter = one_hot((before < lane) | (lane >= LANES))
    odd = ids % 2 == 1
    start = ((ids // 2) * slot + jnp.where(odd, slot - 1, 0)).astype(jnp.float32)
    total = jnp.zeros(ids.shape, jnp.float32)
    targets = []
    for g in range(groups):
        counted = jnp.dot(one_hot(members[g]), counter, preferred_element_type=jnp.float32)
        rank = counted[:, :LANES] + total
        place = start + jnp.where(odd, -rank, rank)
        targets.append(jnp.sum(jnp.where(members[g], place, 0.0), axis=0, keepdims=True))
        total = total + counted[:, LANES:]
    target = jnp.concatenate(targets, axis=0)
    target = target.astype(jnp.int32)
    target_ref[...] = target
    upper = lax.broadcasted_iota(jnp.int32, (HEAD, LANES), 0) < HEAD // 2
    for o in range(owners):
        out_ref[o, planes * slot :, :] = jnp.where(
            upper, total[2 * o : 2 * o + 1, :], total[2 * o + 1 : 2 * o + 2, :]
        ).astype(jnp.bfloat16)
    for copy in rows_copies:
        copy.wait()
    for at in range(0, rows_ref.shape[0], BLOCK):
        turned_ref[:, at : at + BLOCK] = rows_ref[at : at + BLOCK, :].T
    for b in range(owners * slot // BLOCK):
        places = lax.broadcasted_iota(jnp.int32, (BLOCK, LANES), 0) + b * BLOCK
        pick = jnp.concatenate(
            [one_hot(places == target[g : g + 1, :]) for g in range(groups)], axis=1
        )
        sent = lax.dot_general(
            turned_ref[...], pick, (((1,), (1,)), ((), ())), preferred_element_type=jnp.float32
        )
        sent = sent.astype(jnp.bfloat16).T
        first, count = b * BLOCK // slot, BLOCK // slot
        for j in range(planes):
            out_ref[first : first + count, j * slot : (j + 1) * slot, :] = sent[
                :, j * LANES : (j + 1) * LANES
            ].reshape(count, slot, LANES)


def weights(left, right, diagonal):
    scores = lax.dot_general(
        left, right, (((1,), (1,)), ((), ())), preferred_element_type=jnp.float32
    )
    weight = jnp.exp2(scores * (TAU * math.log2(math.e)))
    if diagonal:
        here = lax.broadcasted_iota(jnp.int32, weight.shape, 0)
        there = lax.broadcasted_iota(jnp.int32, weight.shape, 1)
        weight = jnp.where(here == there, 0.0, weight)
    return weight.astype(jnp.bfloat16)


def owner_kernel(
    owners, slot, rows_ref, out_ref, value_ref, left_ref, right_ref, *refs
):
    unit_refs, weight_refs, turned_refs = refs[:2], refs[2:4], refs[4:]
    size, width = value_ref.shape[0], value_ref.shape[1] - LANES
    planes = width // LANES
    part = slot // 2
    side = size // 2
    blocks = side // BLOCK
    spans = [slice(b * BLOCK, (b + 1) * BLOCK) for b in range(2 * blocks)]
    tiles = [slice(at, at + TILE) for at in range(0, side, TILE)]
    counts = [rows_ref[s, planes * slot :, :].astype(jnp.float32) for s in range(owners)]
    most = functools.reduce(jnp.maximum, counts)
    firsts = [c[:1, :] for c in counts]
    seconds = [c[HEAD // 2 : HEAD // 2 + 1, :] for c in counts]

    def plane(h, j):
        at = j * slot + h * part
        return rows_ref[:, at : at + part, :].reshape(side, LANES)

    def write(b, result):
        h, s = b * BLOCK // side, b * BLOCK % side // part
        for i in range(BLOCK // part):
            at = (s + i) * slot + h * part
            out_ref[at : at + part, :] = result[i * part : (i + 1) * part, :]

    each = LANES // part
    lane = lax.broadcasted_iota(jnp.int32, (1, LANES), 1)
    def prepare(h):
        rank = (lane % part).astype(jnp.float32) + h * part
        for g in range(owners // each):
            first, second = firsts[g * each], seconds[g * each]
            for i in range(1, each):
                first = jnp.where(lane < i * part, first, firsts[g * each + i])
                second = jnp.where(lane < i * part, second, seconds[g * each + i])
            there = one_hot((rank < first) | (rank >= slot - second))
            turned_refs[h][width:, g * LANES : (g + 1) * LANES] = jnp.broadcast_to(
                there, (2 * HEAD, LANES)
            )
        wide = [plane(h, j).astype(jnp.float32) for j in range(planes)]
        square = functools.reduce(lambda a, b: a + b, [w * w for w in wide])
        scale = lax.rsqrt(jnp.sum(square, axis=1, keepdims=True) + 1e-06)
        for j in range(planes):
            columns = slice(j * LANES, (j + 1) * LANES)
            unit_refs[h][:, columns] = (wide[j] * scale).astype(jnp.bfloat16)
            turned_refs[h][columns, :] = plane(h, j).T

    def weigh(h):
        units = [unit_refs[h][t, :] for t in tiles]
        for k, across in enumerate(tiles):
            for b, down in enumerate(tiles[: k + 1]):
                weight = weights(units[b], units[k], b == k)
                weight_refs[h][down, across] = weight
                if b != k:
                    weight_refs[h][across, down] = weight.T

    def mix(h):
        turned_ref = turned_refs[h]
        for b in range(blocks):
            total = jnp.dot(
                turned_ref[...], weight_refs[h][:, spans[b]], preferred_element_type=jnp.float32
            )
            result = turned_ref[:width, spans[b]].astype(jnp.float32)
            result = result - total[:width, :] / (1.0 + total[width : width + 1, :])
            write(h * blocks + b, result.astype(jnp.bfloat16).T)

    prepare(0)
    weigh(0)
    prepare(1)
    weigh(1)
    mix(0)
    mix(1)

    @pl.when(jnp.max(most) > part)
    def all_pairs():
        column = lax.broadcasted_iota(jnp.int32, (part, LANES), 1)
        for h in range(2):
            rank = lax.broadcasted_iota(jnp.int32, (part, LANES), 0).astype(jnp.float32) + h * part
            for s in range(owners):
                here = pl.ds(h * side + s * part, part)
                mine = rank < firsts[s]
                there = mine | (rank >= slot - seconds[s])
                sign = jnp.where(mine, 1.0, -1.0)
                left = jnp.where(column == 0, sign, jnp.where(column == 1, 1.0, 0.0))
                right = jnp.where(column == 0, 2.0 * sign, jnp.where(column == 1, -2.0, 0.0))
                left_ref[here, width:] = left.astype(jnp.bfloat16)
                right_ref[here, width:] = right.astype(jnp.bfloat16)
                value_ref[here, width:] = one_hot(there & (column == 0))
            for j in range(planes):
                value_ref[h * side : (h + 1) * side, j * LANES : (j + 1) * LANES] = plane(h, j)
            left_ref[h * side : (h + 1) * side, :width] = unit_refs[h][...]
            right_ref[h * side : (h + 1) * side, :width] = unit_refs[h][...]
        for b in range(2 * blocks):
            total = 0.0
            for k in range(2 * blocks):
                weight = weights(left_ref[spans[b], :], right_ref[spans[k], :], b == k)
                total = total + jnp.dot(
                    weight, value_ref[spans[k], :], preferred_element_type=jnp.float32
                )
            mass = total[:, width : width + 1]
            result = value_ref[spans[b], :width].astype(jnp.float32)
            write(b, (result - total[:, :width] / (1.0 + mass)).astype(jnp.bfloat16))


def return_kernel(target_ref, rows_ref, out_ref, turned_ref, held_ref, leaving):
    target = target_ref[...]
    size, width = rows_ref.shape
    for at in range(0, size, BLOCK):
        turned_ref[:, at : at + BLOCK] = rows_ref[at : at + BLOCK, :].T
    places = lax.broadcasted_iota(jnp.int32, (size, LANES), 0)
    each = TILE // LANES
    copies = copies_of(held_ref, out_ref, leaving)
    ready = len(copies) * TILE // held_ref.shape[0]
    for b in range(held_ref.shape[0] // TILE):
        pick = jnp.concatenate(
            [one_hot(places == target[g : g + 1, :]) for g in range(b * each, (b + 1) * each)],
            axis=1,
        )
        result = jnp.dot(turned_ref[...], pick, preferred_element_type=jnp.float32)
        held_ref[b * TILE : (b + 1) * TILE, :] = result.astype(jnp.bfloat16).T
        for copy in copies[b * ready : (b + 1) * ready]:
            copy.start()
    for copy in copies:
        copy.wait()


VMEM = pl.BlockSpec(memory_space=pltpu.VMEM)
HBM = pl.BlockSpec(memory_space=pltpu.HBM)
PARAMS = pltpu.CompilerParams(vmem_limit_bytes=VMEM_LIMIT)


def on_device(embedding, cluster_of):
    rows_here, width = embedding.shape
    axes = ("tm", "clus")
    owners = lax.axis_size("tm") * lax.axis_size("clus")
    half = lax.axis_size("clus") // 2
    slot = 2 * rows_here // owners
    size = owners * slot
    groups = rows_here // LANES
    padded = width + LANES
    depth = slot * (width // LANES) + HEAD
    outgoing, target = pl.pallas_call(
        functools.partial(route_kernel, owners, slot, half),
        out_shape=(
            jax.ShapeDtypeStruct((owners, depth, LANES), jnp.bfloat16),
            jax.ShapeDtypeStruct((groups, LANES), jnp.int32),
        ),
        in_specs=[HBM, HBM],
        out_specs=(VMEM, VMEM),
        scratch_shapes=[
            pltpu.VMEM((groups, LANES), jnp.int32),
            pltpu.VMEM((rows_here, width), jnp.bfloat16),
            pltpu.VMEM((width, rows_here), jnp.bfloat16),
            pltpu.SemaphoreType.DMA,
            pltpu.SemaphoreType.DMA((4,)),
        ],
        compiler_params=PARAMS,
        name="route",
    )(
        pltpu.with_memory_space_constraint(cluster_of.reshape(groups, LANES), pltpu.HBM),
        pltpu.with_memory_space_constraint(embedding, pltpu.HBM),
    )

    order = [
        start + side * half + low
        for start in range(0, owners, 2 * half)
        for low in range(half)
        for side in range(2)
    ]

    def exchange(rows):
        return lax.all_to_all(
            rows, axes, split_axis=0, concat_axis=0, tiled=True, axis_index_groups=[order]
        )

    arrived = exchange(outgoing)
    answers = pl.pallas_call(
        functools.partial(owner_kernel, owners, slot),
        out_shape=jax.ShapeDtypeStruct((size, width), jnp.bfloat16),
        in_specs=[VMEM],
        out_specs=VMEM,
        scratch_shapes=[pltpu.VMEM((size, padded), jnp.bfloat16)] * 3
        + [pltpu.VMEM((size // 2, width), jnp.bfloat16)] * 2
        + [pltpu.VMEM((size // 2, size // 2), jnp.bfloat16)] * 2
        + [pltpu.VMEM((width + 2 * HEAD, size // 2), jnp.bfloat16)] * 2,
        compiler_params=PARAMS,
        name="pairs",
    )(arrived)
    returned = exchange(answers.reshape(owners, slot, width)).reshape(size, width)
    return pl.pallas_call(
        return_kernel,
        out_shape=jax.ShapeDtypeStruct((rows_here, width), jnp.bfloat16),
        in_specs=[VMEM, VMEM],
        out_specs=pl.BlockSpec(memory_space=pl.ANY),
        scratch_shapes=[
            pltpu.VMEM((width, size), jnp.bfloat16),
            pltpu.VMEM((rows_here, width), jnp.bfloat16),
            pltpu.SemaphoreType.DMA((8,)),
        ],
        compiler_params=PARAMS,
        name="back",
    )(target, returned)


def solution(mesh):
    return jax.shard_map(
        on_device,
        mesh=mesh,
        in_specs=(P(("tm", "clus"), None), P(("tm", "clus"))),
        out_specs=P(("tm", "clus"), None),
        check_vma=False,
    )
```

```python
import functools
import math

import jax
import jax.numpy as jnp
from jax import lax
from jax.experimental import pallas as pl
from jax.experimental.pallas import tpu as pltpu
from jax.sharding import PartitionSpec as P

TAU = 40.0
LANES = 128
HEAD = 8
BLOCK = 512
TILE = 256
VMEM_LIMIT = 32 * 1024 * 1024


def one_hot(mask):
    return jnp.where(mask, 1.0, 0.0).astype(jnp.bfloat16)


def copies_of(source_ref, target_ref, semaphores):
    pieces = semaphores.shape[0]
    each = source_ref.shape[0] // pieces
    spans = [pl.ds(i * each, each) for i in range(pieces)]
    return [
        pltpu.make_async_copy(source_ref.at[span], target_ref.at[span], semaphores.at[i])
        for i, span in enumerate(spans)
    ]


def route_kernel(
    owners, slot, half, cluster_hbm_ref, rows_hbm_ref, out_ref, target_ref,
    cluster_ref, rows_ref, turned_ref, cluster_arrival, rows_arrival,
):
    ids_copy = pltpu.make_async_copy(cluster_hbm_ref, cluster_ref, cluster_arrival)
    ids_copy.start()
    rows_copies = copies_of(rows_hbm_ref, rows_ref, rows_arrival)
    for copy in rows_copies:
        copy.start()
    groups = cluster_ref.shape[0]
    planes = rows_ref.shape[1] // LANES
    ids_copy.wait()
    cluster = cluster_ref[...]
    owner = cluster // 2
    row, side, low = owner // (2 * half), (owner // half) % 2, owner % half
    place = ((row % 2) * half + low) * (owners // (4 * half)) + row // 2
    cluster = 2 * (2 * place + side) + cluster % 2
    ids = lax.broadcasted_iota(jnp.int32, (2 * owners, LANES), 0)
    members = [ids == cluster[g : g + 1, :] for g in range(groups)]
    before = lax.broadcasted_iota(jnp.int32, (LANES, 2 * LANES), 0)
    lane = lax.broadcasted_iota(jnp.int32, (LANES, 2 * LANES), 1)
    counter = one_hot((before < lane) | (lane >= LANES))
    odd = ids % 2 == 1
    start = ((ids // 2) * slot + jnp.where(odd, slot - 1, 0)).astype(jnp.float32)
    total = jnp.zeros(ids.shape, jnp.float32)
    targets = []
    for g in range(groups):
        counted = jnp.dot(one_hot(members[g]), counter, preferred_element_type=jnp.float32)
        rank = counted[:, :LANES] + total
        place = start + jnp.where(odd, -rank, rank)
        targets.append(jnp.sum(jnp.where(members[g], place, 0.0), axis=0, keepdims=True))
        total = total + counted[:, LANES:]
    target = jnp.concatenate(targets, axis=0)
    target = target.astype(jnp.int32)
    target_ref[...] = target
    upper = lax.broadcasted_iota(jnp.int32, (HEAD, LANES), 0) < HEAD // 2
    for o in range(owners):
        out_ref[o, planes * slot :, :] = jnp.where(
            upper, total[2 * o : 2 * o + 1, :], total[2 * o + 1 : 2 * o + 2, :]
        ).astype(jnp.bfloat16)
    for copy in rows_copies:
        copy.wait()
    for at in range(0, rows_ref.shape[0], BLOCK):
        turned_ref[:, at : at + BLOCK] = rows_ref[at : at + BLOCK, :].T
    for b in range(owners * slot // BLOCK):
        places = lax.broadcasted_iota(jnp.int32, (BLOCK, LANES), 0) + b * BLOCK
        pick = jnp.concatenate(
            [one_hot(places == target[g : g + 1, :]) for g in range(groups)], axis=1
        )
        sent = lax.dot_general(
            turned_ref[...], pick, (((1,), (1,)), ((), ())), preferred_element_type=jnp.float32
        )
        sent = sent.astype(jnp.bfloat16).T
        first, count = b * BLOCK // slot, BLOCK // slot
        for j in range(planes):
            out_ref[first : first + count, j * slot : (j + 1) * slot, :] = sent[
                :, j * LANES : (j + 1) * LANES
            ].reshape(count, slot, LANES)


def weights(left, right, diagonal):
    scores = lax.dot_general(
        left, right, (((1,), (1,)), ((), ())), preferred_element_type=jnp.float32
    )
    weight = jnp.exp2(scores * (TAU * math.log2(math.e)))
    if diagonal:
        here = lax.broadcasted_iota(jnp.int32, weight.shape, 0)
        there = lax.broadcasted_iota(jnp.int32, weight.shape, 1)
        weight = jnp.where(here == there, 0.0, weight)
    return weight.astype(jnp.bfloat16)


def owner_kernel(
    owners, slot, rows_ref, out_ref, unit_ref, value_ref, left_ref, right_ref, *refs
):
    size, width = unit_ref.shape
    planes = width // LANES
    part = slot // 2
    side = size // 2
    blocks = side // BLOCK
    spans = [slice(b * BLOCK, (b + 1) * BLOCK) for b in range(2 * blocks)]
    tiles = [slice(at, at + TILE) for at in range(0, side, TILE)]
    counts = [rows_ref[s, planes * slot :, :].astype(jnp.float32) for s in range(owners)]
    most = functools.reduce(jnp.maximum, counts)
    firsts = [c[:1, :] for c in counts]
    seconds = [c[HEAD // 2 : HEAD // 2 + 1, :] for c in counts]

    def plane(h, j):
        at = j * slot + h * part
        return rows_ref[:, at : at + part, :].reshape(side, LANES)

    def write(b, result):
        h, s = b * BLOCK // side, b * BLOCK % side // part
        for i in range(BLOCK // part):
            at = (s + i) * slot + h * part
            out_ref[at : at + part, :] = result[i * part : (i + 1) * part, :]

    each = LANES // part
    lane = lax.broadcasted_iota(jnp.int32, (1, LANES), 1)
    for h in range(2):
        rank = (lane % part).astype(jnp.float32) + h * part
        for g in range(owners // each):
            first, second = firsts[g * each], seconds[g * each]
            for i in range(1, each):
                first = jnp.where(lane < i * part, first, firsts[g * each + i])
                second = jnp.where(lane < i * part, second, seconds[g * each + i])
            there = one_hot((rank < first) | (rank >= slot - second))
            refs[2 + h][width:, g * LANES : (g + 1) * LANES] = jnp.broadcast_to(
                there, (2 * HEAD, LANES)
            )
        wide = [plane(h, j).astype(jnp.float32) for j in range(planes)]
        square = functools.reduce(lambda a, b: a + b, [w * w for w in wide])
        scale = lax.rsqrt(jnp.sum(square, axis=1, keepdims=True) + 1e-06)
        for j in range(planes):
            columns = slice(j * LANES, (j + 1) * LANES)
            unit_ref[h * side : (h + 1) * side, columns] = (wide[j] * scale).astype(jnp.bfloat16)
            refs[2 + h][columns, :] = plane(h, j).T

    for h in range(2):
        weight_ref, turned_ref = refs[h], refs[2 + h]
        units = [unit_ref[h * side + t.start : h * side + t.stop, :] for t in tiles]
        for k, across in enumerate(tiles):
            for b, down in enumerate(tiles[: k + 1]):
                weight = weights(units[b], units[k], b == k)
                weight_ref[down, across] = weight
                if b != k:
                    weight_ref[across, down] = weight.T
        for b in range(blocks):
            total = jnp.dot(
                turned_ref[...], weight_ref[:, spans[b]], preferred_element_type=jnp.float32
            )
            result = turned_ref[:width, spans[b]].astype(jnp.float32)
            result = result - total[:width, :] / (1.0 + total[width : width + 1, :])
            write(h * blocks + b, result.astype(jnp.bfloat16).T)

    @pl.when(jnp.max(most) > part)
    def all_pairs():
        column = lax.broadcasted_iota(jnp.int32, (part, LANES), 1)
        for h in range(2):
            rank = lax.broadcasted_iota(jnp.int32, (part, LANES), 0).astype(jnp.float32) + h * part
            for s in range(owners):
                here = pl.ds(h * side + s * part, part)
                mine = rank < firsts[s]
                there = mine | (rank >= slot - seconds[s])
                sign = jnp.where(mine, 1.0, -1.0)
                left = jnp.where(column == 0, sign, jnp.where(column == 1, 1.0, 0.0))
                right = jnp.where(column == 0, 2.0 * sign, jnp.where(column == 1, -2.0, 0.0))
                left_ref[here, width:] = left.astype(jnp.bfloat16)
                right_ref[here, width:] = right.astype(jnp.bfloat16)
                value_ref[here, width:] = one_hot(there & (column == 0))
            for j in range(planes):
                value_ref[h * side : (h + 1) * side, j * LANES : (j + 1) * LANES] = plane(h, j)
        left_ref[:, :width] = unit_ref[...]
        right_ref[:, :width] = unit_ref[...]
        for b in range(2 * blocks):
            total = 0.0
            for k in range(2 * blocks):
                weight = weights(left_ref[spans[b], :], right_ref[spans[k], :], b == k)
                total = total + jnp.dot(
                    weight, value_ref[spans[k], :], preferred_element_type=jnp.float32
                )
            mass = total[:, width : width + 1]
            result = value_ref[spans[b], :width].astype(jnp.float32)
            write(b, (result - total[:, :width] / (1.0 + mass)).astype(jnp.bfloat16))


def return_kernel(target_ref, rows_ref, out_ref, turned_ref, held_ref, leaving):
    target = target_ref[...]
    size, width = rows_ref.shape
    for at in range(0, size, BLOCK):
        turned_ref[:, at : at + BLOCK] = rows_ref[at : at + BLOCK, :].T
    places = lax.broadcasted_iota(jnp.int32, (size, LANES), 0)
    each = TILE // LANES
    copies = copies_of(held_ref, out_ref, leaving)
    ready = len(copies) * TILE // held_ref.shape[0]
    for b in range(held_ref.shape[0] // TILE):
        pick = jnp.concatenate(
            [one_hot(places == target[g : g + 1, :]) for g in range(b * each, (b + 1) * each)],
            axis=1,
        )
        result = jnp.dot(turned_ref[...], pick, preferred_element_type=jnp.float32)
        held_ref[b * TILE : (b + 1) * TILE, :] = result.astype(jnp.bfloat16).T
        for copy in copies[b * ready : (b + 1) * ready]:
            copy.start()
    for copy in copies:
        copy.wait()


VMEM = pl.BlockSpec(memory_space=pltpu.VMEM)
HBM = pl.BlockSpec(memory_space=pltpu.HBM)
PARAMS = pltpu.CompilerParams(vmem_limit_bytes=VMEM_LIMIT)


def on_device(embedding, cluster_of):
    rows_here, width = embedding.shape
    axes = ("tm", "clus")
    owners = lax.axis_size("tm") * lax.axis_size("clus")
    half = lax.axis_size("clus") // 2
    slot = 2 * rows_here // owners
    size = owners * slot
    groups = rows_here // LANES
    padded = width + LANES
    depth = slot * (width // LANES) + HEAD
    outgoing, target = pl.pallas_call(
        functools.partial(route_kernel, owners, slot, half),
        out_shape=(
            jax.ShapeDtypeStruct((owners, depth, LANES), jnp.bfloat16),
            jax.ShapeDtypeStruct((groups, LANES), jnp.int32),
        ),
        in_specs=[HBM, HBM],
        out_specs=(VMEM, VMEM),
        scratch_shapes=[
            pltpu.VMEM((groups, LANES), jnp.int32),
            pltpu.VMEM((rows_here, width), jnp.bfloat16),
            pltpu.VMEM((width, rows_here), jnp.bfloat16),
            pltpu.SemaphoreType.DMA,
            pltpu.SemaphoreType.DMA((4,)),
        ],
        compiler_params=PARAMS,
        name="route",
    )(
        pltpu.with_memory_space_constraint(cluster_of.reshape(groups, LANES), pltpu.HBM),
        pltpu.with_memory_space_constraint(embedding, pltpu.HBM),
    )

    order = [
        (2 * upper + lower) * 2 * half + side * half + low
        for lower in range(2)
        for low in range(half)
        for upper in range(owners // (4 * half))
        for side in range(2)
    ]

    def exchange(rows):
        return lax.all_to_all(
            rows, axes, split_axis=0, concat_axis=0, tiled=True, axis_index_groups=[order]
        )

    arrived = exchange(outgoing)
    answers = pl.pallas_call(
        functools.partial(owner_kernel, owners, slot),
        out_shape=jax.ShapeDtypeStruct((size, width), jnp.bfloat16),
        in_specs=[VMEM],
        out_specs=VMEM,
        scratch_shapes=[pltpu.VMEM((size, width), jnp.bfloat16)]
        + [pltpu.VMEM((size, padded), jnp.bfloat16)] * 3
        + [pltpu.VMEM((size // 2, size // 2), jnp.bfloat16)] * 2
        + [pltpu.VMEM((width + 2 * HEAD, size // 2), jnp.bfloat16)] * 2,
        compiler_params=PARAMS,
        name="pairs",
    )(arrived)
    returned = exchange(answers.reshape(owners, slot, width)).reshape(size, width)
    return pl.pallas_call(
        return_kernel,
        out_shape=jax.ShapeDtypeStruct((rows_here, width), jnp.bfloat16),
        in_specs=[VMEM, VMEM],
        out_specs=pl.BlockSpec(memory_space=pl.ANY),
        scratch_shapes=[
            pltpu.VMEM((width, size), jnp.bfloat16),
            pltpu.VMEM((rows_here, width), jnp.bfloat16),
            pltpu.SemaphoreType.DMA((8,)),
        ],
        compiler_params=PARAMS,
        name="back",
    )(target, returned)


def solution(mesh):
    return jax.shard_map(
        on_device,
        mesh=mesh,
        in_specs=(P(("tm", "clus"), None), P(("tm", "clus"))),
        out_specs=P(("tm", "clus"), None),
        check_vma=False,
    )
```
